32 devices in a mesh: rows: 8 (over z, x), modes: 4 (over y, core).
Axes of the slice: x: 2, y: 2, z: 4, core: 2. Of those that a mesh axis runs over, the one named last changes fastest.
Arguments:
- snapshots: bfloat16 [1024, 5, 6144], P(None, None, 'rows')
- eigvec: bfloat16 [1024, 256], P('rows', 'modes'), may hold values from -0.1875 to 0.1875
- eigval: float32 [256], replicated, may hold values from 30720 to 245760
- jac_self: bfloat16 [5, 5, 6144], P(None, None, 'rows'), may hold values from -0.5 to 1.5
- jac_off: bfloat16 [6, 5, 5, 6144], P(None, None, None, 'rows'), may hold values from -1 to 1
- neighbor: int32 [6, 6144], P(None, 'rows'), may hold values from 0 to 1279
- send_list: int32 [2, 2048], P(None, 'rows'), may hold values from 0 to 767
- send_count: int32 [2, 8], P(None, 'rows'), may hold values from 1 to 256
- owned_cells: int32 [8], P('rows'), may hold values from 1 to 768, 4608 in all
Outputs:
- test_basis: bfloat16 [256, 5, 6144], P('modes', None, 'rows')
- reduced: float32 [256, 256], P('rows', 'modes')
The draws below stay inside these ranges and needn't reach their ends.
Inputs may be any that keep to these rules, and one draw needn't show every extreme that they name: neighbor[b, c] indexes the extended slots of the cell's own partition: its 768 own slots, then 256 lower ghost slots, then 256 upper ghost slots. `send_list`: entries of partition p's lists are local slots of partition p.
All inputs are finite; a program needn't handle non-finite values. No bound on the sum of `owned_cells` on one device may be relied on, other than what follows from the above.
Results may differ from the reference program's by a relative error of at most 0.0049.
Values may be sent and summed in bfloat16 or wider, within the bound.
A program may use at most 128 MiB of HBM per device.

```python
import math
import jax
import jax.numpy as jnp
import numpy as np
from jax import lax

NVAR = 5
NOFF = 6
NSNAP = 1024
NMODES = 256
C_DEV = 768
HALO = 256
BLOCKS = 8
CELLS = 6144
HALO_ALL = 2048


def draw_snapshots(key, part):
    position = jnp.arange(CELLS, dtype=jnp.float32) / CELLS
    amplitude = 1.0 + 2.0 * position
    values = jax.random.normal(key, (NSNAP, NVAR, CELLS), jnp.float32)
    return (values * amplitude[None, None, :]).astype(jnp.bfloat16)


def draw_send_count(key, part):
    counts = jax.random.randint(key, (2, BLOCKS), 1, HALO + 1)
    chosen = jax.random.randint(jax.random.fold_in(key, 7), (2, 1), 0, BLOCKS)
    spots = jnp.arange(BLOCKS, dtype=jnp.int32)[None, :] == chosen
    return jnp.where(spots, HALO, counts).astype(jnp.int32)


def touch_ends(array, rng, least, top_value):
    longest = array.shape.index(max(array.shape))
    spots = []
    for shift in (0, 1):
        where = [jax.random.randint(jax.random.fold_in(rng, axis), (), 0, length) for axis, length in enumerate(array.shape)]
        where[longest] = (where[longest] + shift) % array.shape[longest]
        spots.append(tuple(where))
    return array.at[spots[0]].set(least).at[spots[1]].set(top_value)


def shard_levels(rng, extent, split, smallest, largest):
    def one(dim, parts):
        heights = jax.random.uniform(jax.random.fold_in(jax.random.fold_in(rng, 6), dim), (parts,), jnp.float32, smallest / len(split), largest / len(split))
        return jnp.repeat(jnp.exp(heights), extent[dim] // parts).reshape((-1,) + (1,) * (len(extent) - dim - 1))

    gain = one(*split[0])
    for cut in split[1:]:
        gain = gain * one(*cut)
    return gain


def split_up(count, total, limit, slope):
    loads = [(1 << 20) // math.isqrt(rank ** slope) + 1 for rank in range(2, count + 1)]
    spare, holding = total - limit - (count - 1), [1] * (count - 1)
    while spare > 0:
        free = [i for i in range(count - 1) if holding[i] < limit]
        whole, left = sum([loads[i] for i in free]), spare
        for i in free:
            extra = min(limit - holding[i], max(1, left * loads[i] // whole), spare)
            holding[i] = holding[i] + extra
            spare = spare - extra
    return np.array([limit] + holding)


def ragged(stream_key, number_of, total, bound, skew):
    if number_of == 2:
        one = jax.random.randint(stream_key, (), max(1, total - bound), min(bound, total - 1) + 1)
        return jnp.stack([one, total - one])
    lengths = jnp.asarray(split_up(number_of, total, bound, skew), jnp.int32)
    twos = (number_of - 1) // 2
    donor, sink = lengths[1:1 + 2 * twos:2], lengths[2:2 + 2 * twos:2]
    room = jnp.minimum(donor - 1, bound - sink)
    passed = jax.random.randint(jax.random.fold_in(stream_key, 1), (twos,), 0, 1 << 20) % (room + 1)
    lengths = lengths.at[1:1 + 2 * twos:2].set(donor - passed).at[2:2 + 2 * twos:2].set(sink + passed)
    return lengths[jax.random.permutation(jax.random.fold_in(stream_key, 2), number_of)]


def normal_values(stream_key, extent, scale, most, pieces=(), kind=jnp.bfloat16):
    result = jax.random.normal(stream_key, extent, jnp.float32) * scale
    if len(pieces) > 0:
        result = shard_levels(stream_key, extent, pieces, -0.22, 0.18) * result
    return jnp.clip(result, min=-most, max=most).astype(kind)


def setup_inputs(seed: int = 0) -> dict:
    splits = jax.random.split(jax.random.key(seed), 10)
    return {
        "snapshots": draw_snapshots(jax.random.fold_in(splits[9], 71), 0),
        "eigvec": normal_values(splits[1], (NSNAP, NMODES), NSNAP ** -0.5, 0.1875, ((0, 8), (1, 4))),
        "eigval": jnp.clip(jnp.exp(jax.random.uniform(splits[2], (NMODES,), jnp.float32, math.log(30720.0), math.log(245760.0))), 30720.0, 245760.0),
        "jac_self": jnp.clip(-0.5 + 2.0 * jax.random.uniform(splits[3], (NVAR, NVAR, CELLS), jnp.float32) ** shard_levels(splits[3], (NVAR, NVAR, CELLS), ((2, 8),), -0.2, 0.2), -0.5, 1.5).astype(jnp.bfloat16),
        "jac_off": normal_values(splits[4], (NOFF, NVAR, NVAR, CELLS), (NVAR * (NOFF + 1)) ** -0.5, 1.0, ((3, 8),)),
        "neighbor": touch_ends(jax.random.randint(splits[5], (NOFF, CELLS), 0, C_DEV + 2 * HALO), jax.random.fold_in(splits[5], 1), 0, (C_DEV + 2 * HALO) - 1).astype(jnp.int32),
        "send_list": touch_ends(jax.random.randint(splits[6], (2, HALO_ALL), 0, C_DEV), jax.random.fold_in(splits[6], 1), 0, C_DEV - 1).astype(jnp.int32),
        "send_count": draw_send_count(jax.random.fold_in(splits[9], 71), 0),
        "owned_cells": ragged(splits[8], BLOCKS, BLOCKS * C_DEV * 3 // 4, C_DEV, 2).astype(jnp.int32),
    }


def reference(snapshots, eigvec, eigval, jac_self, jac_off, neighbor, send_list, send_count, owned_cells):
    snap_count = snapshots.shape[0]
    var_count = snapshots.shape[1]
    cell_count = snapshots.shape[2]
    mode_count = eigvec.shape[1]
    block_count = owned_cells.shape[0]
    cells_dev = cell_count // block_count
    halo_slots = send_list.shape[1] // block_count
    off_count = jac_off.shape[0]
    slot_index = jnp.arange(cell_count, dtype=jnp.int32) % cells_dev
    owned_mask = (slot_index < jnp.repeat(owned_cells, cells_dev)).reshape(1, 1, block_count, cells_dev)
    snap_rows = snapshots.reshape(snap_count, var_count * cell_count)
    products = lax.dot_general(eigvec, snap_rows, (((0,), (0,)), ((), ())), preferred_element_type=jnp.float32)
    products = products.reshape(mode_count, var_count, block_count, cells_dev)
    modes = jnp.where(owned_mask, products, jnp.zeros((), jnp.float32)).astype(jnp.bfloat16)
    send_rows = send_list.reshape(2, block_count, halo_slots)
    part_index = jnp.arange(block_count, dtype=jnp.int32)[:, None]
    live_slots = jnp.arange(halo_slots, dtype=jnp.int32)[None, None, :] < send_count[:, :, None]
    going_down = jnp.where(live_slots[0], modes[:, :, part_index, send_rows[0]], jnp.zeros((), jnp.bfloat16))
    going_up = jnp.where(live_slots[1], modes[:, :, part_index, send_rows[1]], jnp.zeros((), jnp.bfloat16))
    nothing_sent = jnp.zeros_like(going_up[:, :, :1])
    from_below = jnp.concatenate([nothing_sent, going_up[:, :, :-1]], axis=2)
    from_above = jnp.concatenate([going_down[:, :, 1:], nothing_sent], axis=2)
    extended = jnp.concatenate([modes, from_below, from_above], axis=3)
    self_blocks = jac_self.reshape(var_count, var_count, block_count, cells_dev).astype(jnp.float32)
    total = jnp.einsum('vwpc,mwpc->mvpc', self_blocks, modes.astype(jnp.float32))
    near_index = neighbor.reshape(off_count, block_count, cells_dev)
    for off_block in range(off_count):
        gathered = extended[:, :, part_index, near_index[off_block]]
        blocks_here = jac_off[off_block].reshape(var_count, var_count, block_count, cells_dev).astype(jnp.float32)
        total = total + jnp.einsum('vwpc,mwpc->mvpc', blocks_here, gathered.astype(jnp.float32))
    test_basis = jnp.where(owned_mask, total, jnp.zeros((), jnp.float32)).astype(jnp.bfloat16)
    test_basis = test_basis.reshape(mode_count, var_count, cell_count)
    test_rows = test_basis.reshape(mode_count, var_count * cell_count)
    snapshot_products = lax.dot_general(snap_rows, test_rows, (((1,), (1,)), ((), ())), preferred_element_type=jnp.float32)
    scales = 1.0 / jnp.sqrt(eigval)
    reduced = jnp.dot(eigvec.astype(jnp.float32).T, snapshot_products, precision=lax.Precision.HIGHEST)
    reduced = reduced * scales[:, None] * scales[None, :]
    return (test_basis, reduced)
```

```python
import functools

import jax
import jax.numpy as jnp
from jax import lax
from jax.experimental import pallas as pl
from jax.experimental.pallas import tpu as pltpu
from jax.sharding import PartitionSpec as P

MESH = pl.DeviceIdType.MESH
F32 = jnp.float32
BF16 = jnp.bfloat16


def one_hot(index_row, start, depth):
    rows = lax.broadcasted_iota(jnp.int32, (depth, index_row.shape[1]), 0) + start
    return jnp.where(rows == index_row, 1.0, 0.0).astype(BF16)


def kernel(
    count_rows, count_modes,
    snap_hbm, ev_ref, eigval_ref, jself_ref, joff_ref, nbr_ref, slist_ref, scount_ref, owned_ref,
    test_ref, red_ref,
    snap, full, ext, pack, hot_send, hot_own, hot_ghost, near, acc, prod, out_box, in_box,
    snap_sem, ev_send, ev_recv, fan_send, fan_recv, halo_send, halo_recv, red_send, red_recv,
):
    p = lax.axis_index("rows")
    j = lax.axis_index("modes")
    var_count, snap_count, cells = snap.shape
    panel, depth = ev_ref.shape
    off_count = nbr_ref.shape[0]
    halo = slist_ref.shape[1]
    rows_out = red_ref.shape[0]
    half = rows_out // 2

    snap_copies = [
        pltpu.make_async_copy(snap_hbm.at[v], snap.at[v], snap_sem.at[v]) for v in range(var_count)
    ]
    for copy in snap_copies:
        copy.start()

    def row_peer(k):
        return lax.rem(p + k, count_rows)

    def mode_peer(k):
        return lax.rem(j + k, count_modes)

    barrier = pltpu.get_barrier_semaphore()
    for k in range(1, count_rows):
        pl.semaphore_signal(barrier, inc=1, device_id=(row_peer(k), j), device_id_type=MESH)
    for k in range(1, count_modes):
        pl.semaphore_signal(barrier, inc=1, device_id=(p, mode_peer(k)), device_id_type=MESH)
    pl.semaphore_wait(barrier, count_rows + count_modes - 2)

    def panel_slice(panel_index, source):
        return full.at[
            pl.ds(pl.multiple_of(panel_index * panel, panel), panel),
            pl.ds(pl.multiple_of(source * depth, depth), depth),
        ]

    def ev_copy(k, source):
        return pltpu.make_async_remote_copy(
            src_ref=ev_ref, dst_ref=panel_slice(j, source), send_sem=ev_send.at[k - 1],
            recv_sem=ev_recv.at[k - 1], device_id=(row_peer(k), j), device_id_type=MESH,
        )

    for k in range(1, count_rows):
        ev_copy(k, p).start()

    full[
        pl.ds(pl.multiple_of(j * panel, panel), panel), pl.ds(pl.multiple_of(p * depth, depth), depth)
    ] = ev_ref[...]

    slot = lax.broadcasted_iota(jnp.int32, (1, halo), 1)
    for way in range(2):
        picks = jnp.where(slot < scount_ref[way, 0], slist_ref[pl.ds(way, 1), :], -1)
        hot_send[:, way * halo:(way + 1) * halo] = one_hot(picks, 0, cells)

    @pl.loop(0, off_count)
    def _(b):
        picks = nbr_ref[pl.ds(b, 1), :]
        hot_own[b] = one_hot(picks, 0, cells)
        hot_ghost[b] = one_hot(picks, cells, 2 * halo)

    @pl.when(p == 0)
    def _():
        ext[:, cells:cells + halo] = jnp.zeros((var_count * panel, halo), BF16)

    @pl.when(p == count_rows - 1)
    def _():
        ext[:, cells + halo:] = jnp.zeros((var_count * panel, halo), BF16)

    for k in range(1, count_rows):
        ev_copy(k, lax.rem(p + count_rows - k, count_rows)).wait_recv()

    def fan_copy(k, panel_index):
        piece = full.at[pl.ds(pl.multiple_of(panel_index * panel, panel), panel), :]
        return pltpu.make_async_remote_copy(
            src_ref=piece, dst_ref=piece, send_sem=fan_send.at[k - 1], recv_sem=fan_recv.at[k - 1],
            device_id=(p, mode_peer(k)), device_id_type=MESH,
        )

    for k in range(1, count_modes):
        fan_copy(k, j).start()

    live = lax.broadcasted_iota(jnp.int32, (1, cells), 1) < owned_ref[0]

    def halo_copy(v, way):
        start = cells + (1 - way) * halo
        target = p + 1 if way else p - 1
        return pltpu.make_async_remote_copy(
            src_ref=pack.at[way, pl.ds(v * panel, panel), :],
            dst_ref=ext.at[pl.ds(v * panel, panel), pl.ds(start, halo)],
            send_sem=halo_send.at[way, v], recv_sem=halo_recv.at[way, v],
            device_id=(target, j), device_id_type=MESH,
        )

    mine = full[pl.ds(pl.multiple_of(j * panel, panel), panel), :]
    for v in range(var_count):
        snap_copies[v].wait()
        own = jnp.dot(mine, snap[v], preferred_element_type=F32)
        own = jnp.where(live, own, 0.0).astype(BF16)
        ext[v * panel:(v + 1) * panel, :cells] = own
        sent = jnp.dot(own, hot_send[...], preferred_element_type=F32).astype(BF16)
        for way in range(2):
            pack[way, v * panel:(v + 1) * panel, :] = sent[:, way * halo:(way + 1) * halo]

        @pl.when(p < count_rows - 1)
        def _(v=v):
            halo_copy(v, 1).start()

        @pl.when(p > 0)
        def _(v=v):
            halo_copy(v, 0).start()

    @pl.loop(0, off_count)
    def _(b):
        near[b] = jnp.dot(ext[:, :cells], hot_own[b], preferred_element_type=F32).astype(BF16)

    for v in range(var_count):
        total = jnp.zeros((panel, cells), F32)
        for w in range(var_count):
            total = total + (
                jself_ref[v, w:w + 1, :].astype(F32) * ext[w * panel:(w + 1) * panel, :cells].astype(F32)
            )
        acc[v] = total

    @pl.when(p > 0)
    def _():
        for v in range(var_count):
            halo_copy(v, 1).wait_recv()

    @pl.when(p < count_rows - 1)
    def _():
        for v in range(var_count):
            halo_copy(v, 0).wait_recv()

    width = 256 if cells % 256 == 0 else 128

    @pl.loop(0, cells // width)
    def _(tile):
        lanes = pl.ds(pl.multiple_of(tile * width, width), width)
        for b in range(off_count):
            far = jnp.dot(ext[:, cells:], hot_ghost[b, :, lanes], preferred_element_type=F32)
            both = far + near[b, :, lanes].astype(F32)
            for v in range(var_count):
                total = acc[v, :, lanes]
                for w in range(var_count):
                    total = total + (
                        joff_ref[v, w, b:b + 1, lanes].astype(F32) * both[w * panel:(w + 1) * panel]
                    )
                acc[v, :, lanes] = total

    for v in range(var_count):
        test = jnp.where(live, acc[v], 0.0).astype(BF16)
        test_ref[v] = test
        part = lax.dot_general(
            snap[v], test, (((1,), (1,)), ((), ())), preferred_element_type=F32
        )
        if v == 0:
            prod[...] = part
        else:
            prod[...] += part

    for k in range(1, count_modes):
        fan_copy(k, lax.rem(j + count_modes - k, count_modes)).wait_recv()

    high = prod[...].astype(BF16)
    low = (prod[...] - high.astype(F32)).astype(BF16)
    partial = jnp.dot(full[...], high, preferred_element_type=F32) + jnp.dot(
        full[...], low, preferred_element_type=F32
    )
    for d in range(count_rows):
        top = partial[d * rows_out:d * rows_out + half]
        bottom = partial[d * rows_out + half:(d + 1) * rows_out]
        out_box[d] = jnp.concatenate([top, bottom], axis=1)

    def red_copy(k):
        return pltpu.make_async_remote_copy(
            src_ref=out_box.at[row_peer(k)], dst_ref=in_box.at[k - 1], send_sem=red_send.at[k - 1],
            recv_sem=red_recv.at[k - 1], device_id=(row_peer(k), j), device_id_type=MESH,
        )

    for k in range(1, count_rows):
        red_copy(k).start()

    scales = 1.0 / jnp.sqrt(eigval_ref[...])
    mode_count = scales.shape[1]
    first = lax.broadcasted_iota(jnp.int32, (rows_out, mode_count), 0) + p * rows_out
    lane = lax.broadcasted_iota(jnp.int32, (rows_out, mode_count), 1)
    row_scales = jnp.sum(jnp.where(lane == first, scales, 0.0), axis=1, keepdims=True)
    col_scales = jnp.zeros((1, panel), F32)
    for other in range(count_modes):
        col_scales = col_scales + jnp.where(
            j == other, scales[:, other * panel:(other + 1) * panel], 0.0
        )

    for k in range(1, count_rows):
        ev_copy(k, p).wait_send()
    for k in range(1, count_modes):
        fan_copy(k, j).wait_send()

    @pl.when(p < count_rows - 1)
    def _():
        for v in range(var_count):
            halo_copy(v, 1).wait_send()

    @pl.when(p > 0)
    def _():
        for v in range(var_count):
            halo_copy(v, 0).wait_send()

    total = out_box[p]
    for k in range(1, count_rows):
        red_copy(k).wait_recv()
        total = total + in_box[k - 1]
    together = jnp.concatenate([total[:, :panel], total[:, panel:]], axis=0)
    red_ref[...] = together * row_scales * col_scales
    for k in range(1, count_rows):
        red_copy(k).wait_send()


def fused_shards(mesh, snapshots, eigvec, eigval, jac_self, jac_off, neighbor, send_list, send_count, owned_cells):
    count_rows, count_modes = mesh.shape["rows"], mesh.shape["modes"]
    snap_count, var_count, cells = snapshots.shape
    depth, panel = eigvec.shape
    off_count = neighbor.shape[0]
    halo = send_list.shape[1]
    modes = panel * count_modes
    rows_out = modes // count_rows
    whole = pl.BlockSpec(memory_space=pltpu.VMEM)
    scalars = pl.BlockSpec(memory_space=pltpu.SMEM)
    dma = pltpu.SemaphoreType.DMA
    flops = 2 * snap_count * panel * var_count * cells * 2 + 2 * panel * var_count * off_count * cells * (cells + 2 * halo)
    test, reduced = pl.pallas_call(
        functools.partial(kernel, count_rows, count_modes),
        out_shape=(
            jax.ShapeDtypeStruct((var_count, panel, cells), BF16),
            jax.ShapeDtypeStruct((rows_out, panel), F32),
        ),
        in_specs=[pl.BlockSpec(memory_space=pl.ANY)] + [whole] * 6 + [scalars] * 2,
        out_specs=(whole, whole),
        scratch_shapes=[
            pltpu.VMEM((var_count, snap_count, cells), BF16),
            pltpu.VMEM((modes, snap_count), BF16),
            pltpu.VMEM((var_count * panel, cells + 2 * halo), BF16),
            pltpu.VMEM((2, var_count * panel, halo), BF16),
            pltpu.VMEM((cells, 2 * halo), BF16),
            pltpu.VMEM((off_count, cells, cells), BF16),
            pltpu.VMEM((off_count, 2 * halo, cells), BF16),
            pltpu.VMEM((off_count, var_count * panel, cells), BF16),
            pltpu.VMEM((var_count, panel, cells), F32),
            pltpu.VMEM((snap_count, panel), F32),
            pltpu.VMEM((count_rows, rows_out // 2, 2 * panel), F32),
            pltpu.VMEM((count_rows - 1, rows_out // 2, 2 * panel), F32),
            dma((var_count,)),
            dma((count_rows - 1,)),
            dma((count_rows - 1,)),
            dma((count_modes - 1,)),
            dma((count_modes - 1,)),
            dma((2, var_count)),
            dma((2, var_count)),
            dma((count_rows - 1,)),
            dma((count_rows - 1,)),
        ],
        compiler_params=pltpu.CompilerParams(
            collective_id=0, has_side_effects=True, vmem_limit_bytes=48 * 1024 * 1024
        ),
        cost_estimate=pl.CostEstimate(
            flops=flops, bytes_accessed=2 * snap_count * var_count * cells, transcendentals=0
        ),
        name="galerkin",
    )(
        snapshots.transpose(1, 0, 2), eigvec.T, eigval.reshape(1, modes), jac_self,
        jac_off.transpose(1, 2, 0, 3), neighbor, send_list, send_count, owned_cells,
    )
    return test.transpose(1, 0, 2), reduced


def passed_along(value, axis, steps):
    count = lax.axis_size(axis)
    first, last = (max(0, -steps), min(count, count - steps))
    return lax.ppermute(value, axis, [(source, source + steps) for source in range(first, last)])


def take_slots(values, picks):
    chosen = (jnp.arange(values.shape[-1], dtype=jnp.int32)[:, None] == picks[None, :]).astype(BF16)
    return lax.dot_general(
        values, chosen, (((values.ndim - 1,), (0,)), ((), ())), preferred_element_type=F32
    ).astype(BF16)


def plain_shards(snapshots, eigvec, eigval, jac_self, jac_off, neighbor, send_list, send_count, owned_cells):
    snap_count, var_count, cell_count = snapshots.shape
    panel_width = eigvec.shape[1]
    halo_slots = send_list.shape[1]
    snap_rows = snapshots.reshape(snap_count, var_count * cell_count)
    modes_sum = lax.dot_general(
        lax.all_gather(eigvec, "rows", axis=0, tiled=True), snap_rows, (((0,), (0,)), ((), ())),
        preferred_element_type=F32,
    )
    owned_mask = jnp.arange(cell_count, dtype=jnp.int32)[None, None, :] < owned_cells[0]
    modes = jnp.where(
        owned_mask, modes_sum.reshape(panel_width, var_count, cell_count), jnp.zeros((), F32)
    ).astype(BF16)
    picked = take_slots(modes, send_list.reshape(-1)).reshape(panel_width, var_count, 2, halo_slots)
    live_slots = jnp.arange(halo_slots, dtype=jnp.int32)[None, :] < send_count
    picked = jnp.where(live_slots[None, None], picked, jnp.zeros((), BF16))
    from_below = passed_along(picked[:, :, 1], "rows", 1)
    from_above = passed_along(picked[:, :, 0], "rows", -1)
    extended = jnp.concatenate([modes, from_below, from_above], axis=2)
    total = jnp.einsum("vwc,mwc->mvc", jac_self, modes, preferred_element_type=F32)
    for b in range(neighbor.shape[0]):
        near = take_slots(extended, neighbor[b])
        total = total + jnp.einsum("vwc,mwc->mvc", jac_off[b], near, preferred_element_type=F32)
    test_local = jnp.where(owned_mask, total, jnp.zeros((), F32)).astype(BF16)
    products = lax.dot_general(
        snap_rows, test_local.reshape(panel_width, var_count * cell_count), (((1,), (1,)), ((), ())),
        preferred_element_type=F32,
    )
    shares = lax.psum_scatter(products, "rows", scatter_dimension=0, tiled=True)
    eigvec_rows = lax.all_gather(eigvec, "modes", axis=1, tiled=True)
    partial_sum = jnp.dot(eigvec_rows.astype(F32).T, shares, precision=lax.Precision.HIGHEST)
    reduced_part = lax.psum_scatter(partial_sum, "rows", scatter_dimension=0, tiled=True)
    rows_out = reduced_part.shape[0]
    scales = 1.0 / jnp.sqrt(eigval)
    row_scales = lax.dynamic_slice_in_dim(scales, lax.axis_index("rows") * rows_out, rows_out, 0)
    col_scales = lax.dynamic_slice_in_dim(scales, lax.axis_index("modes") * panel_width, panel_width, 0)
    return (test_local, reduced_part * row_scales[:, None] * col_scales[None, :])


def solution(mesh):
    in_specs = (
        P(None, None, "rows"),
        P("rows", "modes"),
        P(),
        P(None, None, "rows"),
        P(None, None, None, "rows"),
        P(None, "rows"),
        P(None, "rows"),
        P(None, "rows"),
        P("rows"),
    )
    out_specs = (P("modes", None, "rows"), P("rows", "modes"))

    def shards(*operands):
        snapshots, eigvec = operands[:2]
        send_list = operands[6]
        depth, panel = eigvec.shape
        rows_out = panel * mesh.shape["modes"] // mesh.shape["rows"]
        fits = (
            depth % 128 == 0 and panel == 64 and rows_out % 16 == 0
            and snapshots.shape[2] % 128 == 0 and send_list.shape[1] % 128 == 0
        )
        return fused_shards(mesh, *operands) if fits else plain_shards(*operands)

    return jax.shard_map(shards, mesh=mesh, in_specs=in_specs, out_specs=out_specs, check_vma=False)
```

```python
import functools

import jax
import jax.numpy as jnp
from jax import lax
from jax.experimental import pallas as pl
from jax.experimental.pallas import tpu as pltpu
from jax.sharding import PartitionSpec as P

MESH = pl.DeviceIdType.MESH
F32 = jnp.float32
BF16 = jnp.bfloat16


def one_hot(index_row, start, depth):
    rows = lax.broadcasted_iota(jnp.int32, (depth, index_row.shape[1]), 0) + start
    return jnp.where(rows == index_row, 1.0, 0.0).astype(BF16)


def kernel(
    count_rows, count_modes,
    snap_hbm, ev_hbm, eigval_hbm, jself_hbm, joff_hbm, nbr_hbm, slist_hbm, scount_hbm, owned_hbm,
    test_hbm, red_ref,
    test_ref, eigval_ref, jself_ref, joff_ref, nbr_ref, slist_ref, scount_ref, owned_ref, snap, full, ext, pack, hot_send, hot_own, hot_ghost, near, acc, prod, out_box, in_box,
    load_sem, test_sem, snap_sem, ev_send, ev_recv, fan_send, fan_recv, halo_send, halo_recv, red_send, red_recv,
):
    p = lax.axis_index("rows")
    j = lax.axis_index("modes")
    var_count, snap_count, cells = snap.shape
    panel, depth = ev_hbm.shape
    off_count = nbr_ref.shape[0]
    halo = slist_ref.shape[1]
    rows_out = red_ref.shape[0]
    half = rows_out // 2

    mine_slice = full.at[
        pl.ds(pl.multiple_of(j * panel, panel), panel), pl.ds(pl.multiple_of(p * depth, depth), depth)
    ]
    loads = [
        pltpu.make_async_copy(source, target, load_sem.at[i])
        for i, (source, target) in enumerate((
            (nbr_hbm, nbr_ref), (slist_hbm, slist_ref), (scount_hbm, scount_ref), (owned_hbm, owned_ref),
            (ev_hbm, mine_slice), (jself_hbm, jself_ref), (joff_hbm, joff_ref), (eigval_hbm, eigval_ref),
        ))
    ]
    for copy in loads:
        copy.start()
    snap_copies = [
        pltpu.make_async_copy(snap_hbm.at[v], snap.at[v], snap_sem.at[v]) for v in range(var_count)
    ]
    for copy in snap_copies:
        copy.start()

    def row_peer(k):
        return lax.rem(p + k, count_rows)

    def mode_peer(k):
        return lax.rem(j + k, count_modes)

    barrier = pltpu.get_barrier_semaphore()
    for k in range(1, count_rows):
        pl.semaphore_signal(barrier, inc=1, device_id=(row_peer(k), j), device_id_type=MESH)
    for k in range(1, count_modes):
        pl.semaphore_signal(barrier, inc=1, device_id=(p, mode_peer(k)), device_id_type=MESH)
    pl.semaphore_wait(barrier, count_rows + count_modes - 2)

    def panel_slice(panel_index, source):
        return full.at[
            pl.ds(pl.multiple_of(panel_index * panel, panel), panel),
            pl.ds(pl.multiple_of(source * depth, depth), depth),
        ]

    def ev_copy(k, source):
        return pltpu.make_async_remote_copy(
            src_ref=ev_hbm, dst_ref=panel_slice(j, source), send_sem=ev_send.at[k - 1],
            recv_sem=ev_recv.at[k - 1], device_id=(row_peer(k), j), device_id_type=MESH,
        )

    for k in range(1, count_rows):
        ev_copy(k, p).start()

    for copy in loads:
        copy.wait()
    slot = lax.broadcasted_iota(jnp.int32, (1, halo), 1)
    for way in range(2):
        picks = jnp.where(slot < scount_ref[0, way], slist_ref[pl.ds(way, 1), :], -1)
        hot_send[:, way * halo:(way + 1) * halo] = one_hot(picks, 0, cells)

    @pl.loop(0, off_count)
    def _(b):
        picks = nbr_ref[pl.ds(b, 1), :]
        hot_own[b] = one_hot(picks, 0, cells)
        hot_ghost[b] = one_hot(picks, cells, 2 * halo)

    @pl.when(p == 0)
    def _():
        ext[:, cells:cells + halo] = jnp.zeros((var_count * panel, halo), BF16)

    @pl.when(p == count_rows - 1)
    def _():
        ext[:, cells + halo:] = jnp.zeros((var_count * panel, halo), BF16)

    for k in range(1, count_rows):
        ev_copy(k, lax.rem(p + count_rows - k, count_rows)).wait_recv()

    def fan_copy(k, panel_index):
        piece = full.at[pl.ds(pl.multiple_of(panel_index * panel, panel), panel), :]
        return pltpu.make_async_remote_copy(
            src_ref=piece, dst_ref=piece, send_sem=fan_send.at[k - 1], recv_sem=fan_recv.at[k - 1],
            device_id=(p, mode_peer(k)), device_id_type=MESH,
        )

    for k in range(1, count_modes):
        fan_copy(k, j).start()

    live = lax.broadcasted_iota(jnp.int32, (1, cells), 1) < owned_ref[0]

    def halo_copy(v, way):
        start = cells + (1 - way) * halo
        target = p + 1 if way else p - 1
        return pltpu.make_async_remote_copy(
            src_ref=pack.at[way, pl.ds(v * panel, panel), :],
            dst_ref=ext.at[pl.ds(v * panel, panel), pl.ds(start, halo)],
            send_sem=halo_send.at[way, v], recv_sem=halo_recv.at[way, v],
            device_id=(target, j), device_id_type=MESH,
        )

    mine = full[pl.ds(pl.multiple_of(j * panel, panel), panel), :]
    for v in range(var_count):
        snap_copies[v].wait()
        own = jnp.dot(mine, snap[v], preferred_element_type=F32)
        own = jnp.where(live, own, 0.0).astype(BF16)
        ext[v * panel:(v + 1) * panel, :cells] = own
        sent = jnp.dot(own, hot_send[...], preferred_element_type=F32).astype(BF16)
        for way in range(2):
            pack[way, v * panel:(v + 1) * panel, :] = sent[:, way * halo:(way + 1) * halo]

        @pl.when(p < count_rows - 1)
        def _(v=v):
            halo_copy(v, 1).start()

        @pl.when(p > 0)
        def _(v=v):
            halo_copy(v, 0).start()

    @pl.loop(0, off_count)
    def _(b):
        near[b] = jnp.dot(ext[:, :cells], hot_own[b], preferred_element_type=F32).astype(BF16)

    for v in range(var_count):
        total = jnp.zeros((panel, cells), F32)
        for w in range(var_count):
            total = total + (
                jself_ref[v, w:w + 1, :].astype(F32) * ext[w * panel:(w + 1) * panel, :cells].astype(F32)
            )
        acc[v] = total

    width = 256 if cells % 256 == 0 else 128

    lots = (range(0, 2), range(2, var_count))
    for lot in lots:
        @pl.when(p > 0)
        def _(lot=lot):
            for v in lot:
                halo_copy(v, 1).wait_recv()

        @pl.when(p < count_rows - 1)
        def _(lot=lot):
            for v in lot:
                halo_copy(v, 0).wait_recv()

        rows = slice(lot[0] * panel, (lot[-1] + 1) * panel)

        @pl.loop(0, cells // width)
        def _(tile, lot=lot, rows=rows):
            lanes = pl.ds(pl.multiple_of(tile * width, width), width)
            for b in range(off_count):
                far = jnp.dot(ext[rows, cells:], hot_ghost[b, :, lanes], preferred_element_type=F32)
                both = far + near[b, rows, lanes].astype(F32)
                for v in range(var_count):
                    total = acc[v, :, lanes]
                    for i, w in enumerate(lot):
                        total = total + (
                            joff_ref[v, w, b:b + 1, lanes].astype(F32) * both[i * panel:(i + 1) * panel]
                        )
                    acc[v, :, lanes] = total

    for v in range(var_count):
        test = jnp.where(live, acc[v], 0.0).astype(BF16)
        test_ref[v] = test
        pltpu.make_async_copy(test_ref.at[v], test_hbm.at[v], test_sem.at[v]).start()
        part = lax.dot_general(
            snap[v], test, (((1,), (1,)), ((), ())), preferred_element_type=F32
        )
        if v == 0:
            prod[...] = part
        else:
            prod[...] += part

    for k in range(1, count_modes):
        fan_copy(k, lax.rem(j + count_modes - k, count_modes)).wait_recv()

    high = prod[...].astype(BF16)
    low = (prod[...] - high.astype(F32)).astype(BF16)
    partial = jnp.dot(full[...], high, preferred_element_type=F32) + jnp.dot(
        full[...], low, preferred_element_type=F32
    )
    for d in range(count_rows):
        top = partial[d * rows_out:d * rows_out + half]
        bottom = partial[d * rows_out + half:(d + 1) * rows_out]
        out_box[d] = jnp.concatenate([top, bottom], axis=1)

    def red_copy(k):
        return pltpu.make_async_remote_copy(
            src_ref=out_box.at[row_peer(k)], dst_ref=in_box.at[k - 1], send_sem=red_send.at[k - 1],
            recv_sem=red_recv.at[k - 1], device_id=(row_peer(k), j), device_id_type=MESH,
        )

    for k in range(1, count_rows):
        red_copy(k).start()

    scales = 1.0 / jnp.sqrt(eigval_ref[...])
    mode_count = scales.shape[1]
    first = lax.broadcasted_iota(jnp.int32, (rows_out, mode_count), 0) + p * rows_out
    lane = lax.broadcasted_iota(jnp.int32, (rows_out, mode_count), 1)
    row_scales = jnp.sum(jnp.where(lane == first, scales, 0.0), axis=1, keepdims=True)
    col_scales = jnp.zeros((1, panel), F32)
    for other in range(count_modes):
        col_scales = col_scales + jnp.where(
            j == other, scales[:, other * panel:(other + 1) * panel], 0.0
        )

    for k in range(1, count_rows):
        ev_copy(k, p).wait_send()
    for k in range(1, count_modes):
        fan_copy(k, j).wait_send()

    @pl.when(p < count_rows - 1)
    def _():
        for v in range(var_count):
            halo_copy(v, 1).wait_send()

    @pl.when(p > 0)
    def _():
        for v in range(var_count):
            halo_copy(v, 0).wait_send()

    for v in range(var_count):
        pltpu.make_async_copy(test_ref.at[v], test_hbm.at[v], test_sem.at[v]).wait()

    total = out_box[p]
    for k in range(1, count_rows):
        red_copy(k).wait_recv()
        total = total + in_box[k - 1]
    together = jnp.concatenate([total[:, :panel], total[:, panel:]], axis=0)
    red_ref[...] = together * row_scales * col_scales
    for k in range(1, count_rows):
        red_copy(k).wait_send()


def fused_shards(mesh, snapshots, eigvec, eigval, jac_self, jac_off, neighbor, send_list, send_count, owned_cells):
    count_rows, count_modes = mesh.shape["rows"], mesh.shape["modes"]
    snap_count, var_count, cells = snapshots.shape
    depth, panel = eigvec.shape
    off_count = neighbor.shape[0]
    halo = send_list.shape[1]
    modes = panel * count_modes
    rows_out = modes // count_rows
    whole = pl.BlockSpec(memory_space=pltpu.VMEM)
    dma = pltpu.SemaphoreType.DMA
    flops = 2 * snap_count * panel * var_count * cells * 2 + 2 * panel * var_count * off_count * cells * (cells + 2 * halo)
    test, reduced = pl.pallas_call(
        functools.partial(kernel, count_rows, count_modes),
        out_shape=(
            jax.ShapeDtypeStruct((var_count, panel, cells), BF16),
            jax.ShapeDtypeStruct((rows_out, panel), F32),
        ),
        in_specs=[pl.BlockSpec(memory_space=pl.ANY)] * 9,
        out_specs=(pl.BlockSpec(memory_space=pl.ANY), whole),
        scratch_shapes=[
            pltpu.VMEM((var_count, panel, cells), BF16),
            pltpu.VMEM((1, modes), F32),
            pltpu.VMEM(jac_self.shape, BF16),
            pltpu.VMEM((var_count, var_count, off_count, cells), BF16),
            pltpu.VMEM(neighbor.shape, jnp.int32),
            pltpu.VMEM(send_list.shape, jnp.int32),
            pltpu.SMEM((1, 2), jnp.int32),
            pltpu.SMEM((1,), jnp.int32),
            pltpu.VMEM((var_count, snap_count, cells), BF16),
            pltpu.VMEM((modes, snap_count), BF16),
            pltpu.VMEM((var_count * panel, cells + 2 * halo), BF16),
            pltpu.VMEM((2, var_count * panel, halo), BF16),
            pltpu.VMEM((cells, 2 * halo), BF16),
            pltpu.VMEM((off_count, cells, cells), BF16),
            pltpu.VMEM((off_count, 2 * halo, cells), BF16),
            pltpu.VMEM((off_count, var_count * panel, cells), BF16),
            pltpu.VMEM((var_count, panel, cells), F32),
            pltpu.VMEM((snap_count, panel), F32),
            pltpu.VMEM((count_rows, rows_out // 2, 2 * panel), F32),
            pltpu.VMEM((count_rows - 1, rows_out // 2, 2 * panel), F32),
            dma((8,)),
            dma((var_count,)),
            dma((var_count,)),
            dma((count_rows - 1,)),
            dma((count_rows - 1,)),
            dma((count_modes - 1,)),
            dma((count_modes - 1,)),
            dma((2, var_count)),
            dma((2, var_count)),
            dma((count_rows - 1,)),
            dma((count_rows - 1,)),
        ],
        compiler_params=pltpu.CompilerParams(
            collective_id=0, has_side_effects=True, vmem_limit_bytes=58 * 1024 * 1024
        ),
        cost_estimate=pl.CostEstimate(
            flops=flops, bytes_accessed=2 * snap_count * var_count * cells, transcendentals=0
        ),
        name="galerkin",
    )(
        snapshots.transpose(1, 0, 2), eigvec.T, eigval.reshape(1, modes), jac_self,
        jac_off.transpose(1, 2, 0, 3), neighbor, send_list, send_count.T, owned_cells,
    )
    return test.transpose(1, 0, 2), reduced


def passed_along(value, axis, steps):
    count = lax.axis_size(axis)
    first, last = (max(0, -steps), min(count, count - steps))
    return lax.ppermute(value, axis, [(source, source + steps) for source in range(first, last)])


def take_slots(values, picks):
    chosen = (jnp.arange(values.shape[-1], dtype=jnp.int32)[:, None] == picks[None, :]).astype(BF16)
    return lax.dot_general(
        values, chosen, (((values.ndim - 1,), (0,)), ((), ())), preferred_element_type=F32
    ).astype(BF16)


def plain_shards(snapshots, eigvec, eigval, jac_self, jac_off, neighbor, send_list, send_count, owned_cells):
    snap_count, var_count, cell_count = snapshots.shape
    panel_width = eigvec.shape[1]
    halo_slots = send_list.shape[1]
    snap_rows = snapshots.reshape(snap_count, var_count * cell_count)
    modes_sum = lax.dot_general(
        lax.all_gather(eigvec, "rows", axis=0, tiled=True), snap_rows, (((0,), (0,)), ((), ())),
        preferred_element_type=F32,
    )
    owned_mask = jnp.arange(cell_count, dtype=jnp.int32)[None, None, :] < owned_cells[0]
    modes = jnp.where(
        owned_mask, modes_sum.reshape(panel_width, var_count, cell_count), jnp.zeros((), F32)
    ).astype(BF16)
    picked = take_slots(modes, send_list.reshape(-1)).reshape(panel_width, var_count, 2, halo_slots)
    live_slots = jnp.arange(halo_slots, dtype=jnp.int32)[None, :] < send_count
    picked = jnp.where(live_slots[None, None], picked, jnp.zeros((), BF16))
    from_below = passed_along(picked[:, :, 1], "rows", 1)
    from_above = passed_along(picked[:, :, 0], "rows", -1)
    extended = jnp.concatenate([modes, from_below, from_above], axis=2)
    total = jnp.einsum("vwc,mwc->mvc", jac_self, modes, preferred_element_type=F32)
    for b in range(neighbor.shape[0]):
        near = take_slots(extended, neighbor[b])
        total = total + jnp.einsum("vwc,mwc->mvc", jac_off[b], near, preferred_element_type=F32)
    test_local = jnp.where(owned_mask, total, jnp.zeros((), F32)).astype(BF16)
    products = lax.dot_general(
        snap_rows, test_local.reshape(panel_width, var_count * cell_count), (((1,), (1,)), ((), ())),
        preferred_element_type=F32,
    )
    shares = lax.psum_scatter(products, "rows", scatter_dimension=0, tiled=True)
    eigvec_rows = lax.all_gather(eigvec, "modes", axis=1, tiled=True)
    partial_sum = jnp.dot(eigvec_rows.astype(F32).T, shares, precision=lax.Precision.HIGHEST)
    reduced_part = lax.psum_scatter(partial_sum, "rows", scatter_dimension=0, tiled=True)
    rows_out = reduced_part.shape[0]
    scales = 1.0 / jnp.sqrt(eigval)
    row_scales = lax.dynamic_slice_in_dim(scales, lax.axis_index("rows") * rows_out, rows_out, 0)
    col_scales = lax.dynamic_slice_in_dim(scales, lax.axis_index("modes") * panel_width, panel_width, 0)
    return (test_local, reduced_part * row_scales[:, None] * col_scales[None, :])


def solution(mesh):
    in_specs = (
        P(None, None, "rows"),
        P("rows", "modes"),
        P(),
        P(None, None, "rows"),
        P(None, None, None, "rows"),
        P(None, "rows"),
        P(None, "rows"),
        P(None, "rows"),
        P("rows"),
    )
    out_specs = (P("modes", None, "rows"), P("rows", "modes"))

    def shards(*operands):
        snapshots, eigvec = operands[:2]
        send_list = operands[6]
        depth, panel = eigvec.shape
        rows_out = panel * mesh.shape["modes"] // mesh.shape["rows"]
        fits = (
            depth % 128 == 0 and panel == 64 and rows_out % 16 == 0
            and snapshots.shape[2] % 128 == 0 and send_list.shape[1] % 128 == 0
        )
        return fused_shards(mesh, *operands) if fits else plain_shards(*operands)

    return jax.shard_map(shards, mesh=mesh, in_specs=in_specs, out_specs=out_specs, check_vma=False)
```

```python
import functools

import jax
import jax.numpy as jnp
from jax import lax
from jax.experimental import pallas as pl
from jax.experimental.pallas import tpu as pltpu
from jax.sharding import PartitionSpec as P

MESH = pl.DeviceIdType.MESH
F32 = jnp.float32
BF16 = jnp.bfloat16


def one_hot(index_row, start, depth):
    rows = lax.broadcasted_iota(jnp.int32, (depth, index_row.shape[1]), 0) + start
    return jnp.where(rows == index_row, 1.0, 0.0).astype(BF16)


def kernel(
    count_rows, count_modes,
    snap_hbm, ev_hbm, eigval_hbm, jself_hbm, joff_hbm, nbr_hbm, slist_hbm, scount_hbm, owned_hbm,
    test_hbm, red_ref,
    test_ref, eigval_ref, jself_ref, joff_ref, nbr_ref, slist_ref, scount_ref, owned_ref, snap, full, ext, pack, hot_send, hot_own, hot_ghost, near, acc, out_box, in_box,
    load_sem, test_sem, snap_sem, ev_send, ev_recv, fan_send, fan_recv, halo_send, halo_recv, red_send, red_recv,
):
    p = lax.axis_index("rows")
    j = lax.axis_index("modes")
    var_count, snap_count, cells = snap.shape
    panel, depth = ev_hbm.shape
    off_count = nbr_ref.shape[0]
    halo = slist_ref.shape[1]
    rows_out = red_ref.shape[0]
    half = rows_out // 2

    mine_slice = full.at[
        pl.ds(pl.multiple_of(j * panel, panel), panel), pl.ds(pl.multiple_of(p * depth, depth), depth)
    ]
    loads = [
        pltpu.make_async_copy(source, target, load_sem.at[i])
        for i, (source, target) in enumerate((
            (nbr_hbm, nbr_ref), (slist_hbm, slist_ref), (scount_hbm, scount_ref), (owned_hbm, owned_ref),
            (ev_hbm, mine_slice), (jself_hbm, jself_ref), (joff_hbm, joff_ref), (eigval_hbm, eigval_ref),
        ))
    ]
    for copy in loads:
        copy.start()
    snap_copies = [
        pltpu.make_async_copy(snap_hbm.at[v], snap.at[v], snap_sem.at[v]) for v in range(var_count)
    ]
    for copy in snap_copies:
        copy.start()

    def row_peer(k):
        return lax.rem(p + k, count_rows)

    def mode_peer(k):
        return lax.rem(j + k, count_modes)

    barrier = pltpu.get_barrier_semaphore()
    for k in range(1, count_rows):
        pl.semaphore_signal(barrier, inc=1, device_id=(row_peer(k), j), device_id_type=MESH)
    for k in range(1, count_modes):
        pl.semaphore_signal(barrier, inc=1, device_id=(p, mode_peer(k)), device_id_type=MESH)
    pl.semaphore_wait(barrier, count_rows + count_modes - 2)

    def panel_slice(panel_index, source):
        return full.at[
            pl.ds(pl.multiple_of(panel_index * panel, panel), panel),
            pl.ds(pl.multiple_of(source * depth, depth), depth),
        ]

    def ev_copy(k, source):
        return pltpu.make_async_remote_copy(
            src_ref=ev_hbm, dst_ref=panel_slice(j, source), send_sem=ev_send.at[k - 1],
            recv_sem=ev_recv.at[k - 1], device_id=(row_peer(k), j), device_id_type=MESH,
        )

    for k in range(1, count_rows):
        ev_copy(k, p).start()

    for copy in loads:
        copy.wait()
    slot = lax.broadcasted_iota(jnp.int32, (1, halo), 1)
    for way in range(2):
        picks = jnp.where(slot < scount_ref[0, way], slist_ref[pl.ds(way, 1), :], -1)
        hot_send[:, way * halo:(way + 1) * halo] = one_hot(picks, 0, cells)

    @pl.loop(0, off_count)
    def _(b):
        picks = nbr_ref[pl.ds(b, 1), :]
        hot_own[b] = one_hot(picks, 0, cells)
        hot_ghost[b] = one_hot(picks, cells, 2 * halo)

    @pl.when(p == 0)
    def _():
        ext[:, cells:cells + halo] = jnp.zeros((var_count * panel, halo), BF16)

    @pl.when(p == count_rows - 1)
    def _():
        ext[:, cells + halo:] = jnp.zeros((var_count * panel, halo), BF16)

    for k in range(1, count_rows):
        ev_copy(k, lax.rem(p + count_rows - k, count_rows)).wait_recv()

    def fan_copy(k, panel_index):
        piece = full.at[pl.ds(pl.multiple_of(panel_index * panel, panel), panel), :]
        return pltpu.make_async_remote_copy(
            src_ref=piece, dst_ref=piece, send_sem=fan_send.at[k - 1], recv_sem=fan_recv.at[k - 1],
            device_id=(p, mode_peer(k)), device_id_type=MESH,
        )

    for k in range(1, count_modes):
        fan_copy(k, j).start()

    live = lax.broadcasted_iota(jnp.int32, (1, cells), 1) < owned_ref[0]

    def halo_copy(v, way):
        start = cells + (1 - way) * halo
        target = p + 1 if way else p - 1
        return pltpu.make_async_remote_copy(
            src_ref=pack.at[way, pl.ds(v * panel, panel), :],
            dst_ref=ext.at[pl.ds(v * panel, panel), pl.ds(start, halo)],
            send_sem=halo_send.at[way, v], recv_sem=halo_recv.at[way, v],
            device_id=(target, j), device_id_type=MESH,
        )

    mine = full[pl.ds(pl.multiple_of(j * panel, panel), panel), :]
    lots = (range(0, 2), range(2, var_count))
    for lot in lots:
        for v in lot:
            snap_copies[v].wait()
            own = jnp.dot(mine, snap[v], preferred_element_type=F32)
            ext[v * panel:(v + 1) * panel, :cells] = jnp.where(live, own, 0.0).astype(BF16)
        rows = slice(lot[0] * panel, (lot[-1] + 1) * panel)
        sent = jnp.dot(ext[rows, :cells], hot_send[...], preferred_element_type=F32).astype(BF16)
        for way in range(2):
            pack[way, rows, :] = sent[:, way * halo:(way + 1) * halo]

        @pl.when(p < count_rows - 1)
        def _(lot=lot):
            for v in lot:
                halo_copy(v, 1).start()

        @pl.when(p > 0)
        def _(lot=lot):
            for v in lot:
                halo_copy(v, 0).start()

    @pl.loop(0, off_count)
    def _(b):
        near[b] = jnp.dot(ext[:, :cells], hot_own[b], preferred_element_type=F32).astype(BF16)

    for v in range(var_count):
        total = jnp.zeros((panel, cells), F32)
        for w in range(var_count):
            total = total + (
                jself_ref[v, w:w + 1, :].astype(F32) * ext[w * panel:(w + 1) * panel, :cells].astype(F32)
            )
        acc[v] = total

    width = 256 if cells % 256 == 0 else 128

    for lot in lots:
        @pl.when(p > 0)
        def _(lot=lot):
            for v in lot:
                halo_copy(v, 1).wait_recv()

        @pl.when(p < count_rows - 1)
        def _(lot=lot):
            for v in lot:
                halo_copy(v, 0).wait_recv()

        rows = slice(lot[0] * panel, (lot[-1] + 1) * panel)

        @pl.loop(0, cells // width)
        def _(tile, lot=lot, rows=rows):
            lanes = pl.ds(pl.multiple_of(tile * width, width), width)
            for b in range(off_count):
                far = jnp.dot(ext[rows, cells:], hot_ghost[b, :, lanes], preferred_element_type=F32)
                both = far + near[b, rows, lanes].astype(F32)
                for v in range(var_count):
                    total = acc[v, :, lanes]
                    for i, w in enumerate(lot):
                        total = total + (
                            joff_ref[v, w, b:b + 1, lanes].astype(F32) * both[i * panel:(i + 1) * panel]
                        )
                    acc[v, :, lanes] = total

    for v in range(var_count):
        test = jnp.where(live, acc[v], 0.0).astype(BF16)
        test_ref[v] = test
        pltpu.make_async_copy(test_ref.at[v], test_hbm.at[v], test_sem.at[v]).start()
        part = lax.dot_general(
            snap[v], test, (((1,), (1,)), ((), ())), preferred_element_type=F32
        )
        products = part if v == 0 else products + part

    for k in range(1, count_modes):
        fan_copy(k, lax.rem(j + count_modes - k, count_modes)).wait_recv()

    high = products.astype(BF16)
    low = (products - high.astype(F32)).astype(BF16)
    split = jnp.dot(
        full[...], jnp.concatenate([high, low], axis=1), preferred_element_type=F32
    )
    partial = split[:, :panel] + split[:, panel:]
    for d in range(count_rows):
        top = partial[d * rows_out:d * rows_out + half]
        bottom = partial[d * rows_out + half:(d + 1) * rows_out]
        out_box[d] = jnp.concatenate([top, bottom], axis=1)

    def red_copy(k):
        return pltpu.make_async_remote_copy(
            src_ref=out_box.at[row_peer(k)], dst_ref=in_box.at[k - 1], send_sem=red_send.at[k - 1],
            recv_sem=red_recv.at[k - 1], device_id=(row_peer(k), j), device_id_type=MESH,
        )

    for k in range(1, count_rows):
        red_copy(k).start()

    scales = 1.0 / jnp.sqrt(eigval_ref[...])
    mode_count = scales.shape[1]
    first = lax.broadcasted_iota(jnp.int32, (rows_out, mode_count), 0) + p * rows_out
    lane = lax.broadcasted_iota(jnp.int32, (rows_out, mode_count), 1)
    row_scales = jnp.sum(jnp.where(lane == first, scales, 0.0), axis=1, keepdims=True)
    col_scales = jnp.zeros((1, panel), F32)
    for other in range(count_modes):
        col_scales = col_scales + jnp.where(
            j == other, scales[:, other * panel:(other + 1) * panel], 0.0
        )

    for k in range(1, count_rows):
        ev_copy(k, p).wait_send()
    for k in range(1, count_modes):
        fan_copy(k, j).wait_send()

    @pl.when(p < count_rows - 1)
    def _():
        for v in range(var_count):
            halo_copy(v, 1).wait_send()

    @pl.when(p > 0)
    def _():
        for v in range(var_count):
            halo_copy(v, 0).wait_send()

    for v in range(var_count):
        pltpu.make_async_copy(test_ref.at[v], test_hbm.at[v], test_sem.at[v]).wait()

    total = out_box[p]
    for k in range(1, count_rows):
        red_copy(k).wait_recv()
        total = total + in_box[k - 1]
    together = jnp.concatenate([total[:, :panel], total[:, panel:]], axis=0)
    red_ref[...] = together * row_scales * col_scales
    for k in range(1, count_rows):
        red_copy(k).wait_send()


def fused_shards(mesh, snapshots, eigvec, eigval, jac_self, jac_off, neighbor, send_list, send_count, owned_cells):
    count_rows, count_modes = mesh.shape["rows"], mesh.shape["modes"]
    snap_count, var_count, cells = snapshots.shape
    depth, panel = eigvec.shape
    off_count = neighbor.shape[0]
    halo = send_list.shape[1]
    modes = panel * count_modes
    rows_out = modes // count_rows
    whole = pl.BlockSpec(memory_space=pltpu.VMEM)
    dma = pltpu.SemaphoreType.DMA
    flops = 2 * snap_count * panel * var_count * cells * 2 + 2 * panel * var_count * off_count * cells * (cells + 2 * halo)
    test, reduced = pl.pallas_call(
        functools.partial(kernel, count_rows, count_modes),
        out_shape=(
            jax.ShapeDtypeStruct((var_count, panel, cells), BF16),
            jax.ShapeDtypeStruct((rows_out, panel), F32),
        ),
        in_specs=[pl.BlockSpec(memory_space=pl.ANY)] * 9,
        out_specs=(pl.BlockSpec(memory_space=pl.ANY), whole),
        scratch_shapes=[
            pltpu.VMEM((var_count, panel, cells), BF16),
            pltpu.VMEM((1, modes), F32),
            pltpu.VMEM(jac_self.shape, BF16),
            pltpu.VMEM((var_count, var_count, off_count, cells), BF16),
            pltpu.VMEM(neighbor.shape, jnp.int32),
            pltpu.VMEM(send_list.shape, jnp.int32),
            pltpu.SMEM((1, 2), jnp.int32),
            pltpu.SMEM((1,), jnp.int32),
            pltpu.VMEM((var_count, snap_count, cells), BF16),
            pltpu.VMEM((modes, snap_count), BF16),
            pltpu.VMEM((var_count * panel, cells + 2 * halo), BF16),
            pltpu.VMEM((2, var_count * panel, halo), BF16),
            pltpu.VMEM((cells, 2 * halo), BF16),
            pltpu.VMEM((off_count, cells, cells), BF16),
            pltpu.VMEM((off_count, 2 * halo, cells), BF16),
            pltpu.VMEM((off_count, var_count * panel, cells), BF16),
            pltpu.VMEM((var_count, panel, cells), F32),
            pltpu.VMEM((count_rows, rows_out // 2, 2 * panel), F32),
            pltpu.VMEM((count_rows - 1, rows_out // 2, 2 * panel), F32),
            dma((8,)),
            dma((var_count,)),
            dma((var_count,)),
            dma((count_rows - 1,)),
            dma((count_rows - 1,)),
            dma((count_modes - 1,)),
            dma((count_modes - 1,)),
            dma((2, var_count)),
            dma((2, var_count)),
            dma((count_rows - 1,)),
            dma((count_rows - 1,)),
        ],
        compiler_params=pltpu.CompilerParams(
            collective_id=0, has_side_effects=True, vmem_limit_bytes=58 * 1024 * 1024
        ),
        cost_estimate=pl.CostEstimate(
            flops=flops, bytes_accessed=2 * snap_count * var_count * cells, transcendentals=0
        ),
        name="galerkin",
    )(
        snapshots.transpose(1, 0, 2), eigvec.T, eigval.reshape(1, modes), jac_self,
        jac_off.transpose(1, 2, 0, 3), neighbor, send_list, send_count.T, owned_cells,
    )
    return test.transpose(1, 0, 2), reduced


def passed_along(value, axis, steps):
    count = lax.axis_size(axis)
    first, last = (max(0, -steps), min(count, count - steps))
    return lax.ppermute(value, axis, [(source, source + steps) for source in range(first, last)])


def take_slots(values, picks):
    chosen = (jnp.arange(values.shape[-1], dtype=jnp.int32)[:, None] == picks[None, :]).astype(BF16)
    return lax.dot_general(
        values, chosen, (((values.ndim - 1,), (0,)), ((), ())), preferred_element_type=F32
    ).astype(BF16)


def plain_shards(snapshots, eigvec, eigval, jac_self, jac_off, neighbor, send_list, send_count, owned_cells):
    snap_count, var_count, cell_count = snapshots.shape
    panel_width = eigvec.shape[1]
    halo_slots = send_list.shape[1]
    snap_rows = snapshots.reshape(snap_count, var_count * cell_count)
    modes_sum = lax.dot_general(
        lax.all_gather(eigvec, "rows", axis=0, tiled=True), snap_rows, (((0,), (0,)), ((), ())),
        preferred_element_type=F32,
    )
    owned_mask = jnp.arange(cell_count, dtype=jnp.int32)[None, None, :] < owned_cells[0]
    modes = jnp.where(
        owned_mask, modes_sum.reshape(panel_width, var_count, cell_count), jnp.zeros((), F32)
    ).astype(BF16)
    picked = take_slots(modes, send_list.reshape(-1)).reshape(panel_width, var_count, 2, halo_slots)
    live_slots = jnp.arange(halo_slots, dtype=jnp.int32)[None, :] < send_count
    picked = jnp.where(live_slots[None, None], picked, jnp.zeros((), BF16))
    from_below = passed_along(picked[:, :, 1], "rows", 1)
    from_above = passed_along(picked[:, :, 0], "rows", -1)
    extended = jnp.concatenate([modes, from_below, from_above], axis=2)
    total = jnp.einsum("vwc,mwc->mvc", jac_self, modes, preferred_element_type=F32)
    for b in range(neighbor.shape[0]):
        near = take_slots(extended, neighbor[b])
        total = total + jnp.einsum("vwc,mwc->mvc", jac_off[b], near, preferred_element_type=F32)
    test_local = jnp.where(owned_mask, total, jnp.zeros((), F32)).astype(BF16)
    products = lax.dot_general(
        snap_rows, test_local.reshape(panel_width, var_count * cell_count), (((1,), (1,)), ((), ())),
        preferred_element_type=F32,
    )
    shares = lax.psum_scatter(products, "rows", scatter_dimension=0, tiled=True)
    eigvec_rows = lax.all_gather(eigvec, "modes", axis=1, tiled=True)
    partial_sum = jnp.dot(eigvec_rows.astype(F32).T, shares, precision=lax.Precision.HIGHEST)
    reduced_part = lax.psum_scatter(partial_sum, "rows", scatter_dimension=0, tiled=True)
    rows_out = reduced_part.shape[0]
    scales = 1.0 / jnp.sqrt(eigval)
    row_scales = lax.dynamic_slice_in_dim(scales, lax.axis_index("rows") * rows_out, rows_out, 0)
    col_scales = lax.dynamic_slice_in_dim(scales, lax.axis_index("modes") * panel_width, panel_width, 0)
    return (test_local, reduced_part * row_scales[:, None] * col_scales[None, :])


def solution(mesh):
    in_specs = (
        P(None, None, "rows"),
        P("rows", "modes"),
        P(),
        P(None, None, "rows"),
        P(None, None, None, "rows"),
        P(None, "rows"),
        P(None, "rows"),
        P(None, "rows"),
        P("rows"),
    )
    out_specs = (P("modes", None, "rows"), P("rows", "modes"))

    def shards(*operands):
        snapshots, eigvec = operands[:2]
        send_list = operands[6]
        depth, panel = eigvec.shape
        rows_out = panel * mesh.shape["modes"] // mesh.shape["rows"]
        fits = (
            depth % 128 == 0 and panel == 64 and rows_out % 16 == 0
            and snapshots.shape[2] % 128 == 0 and send_list.shape[1] % 128 == 0
        )
        return fused_shards(mesh, *operands) if fits else plain_shards(*operands)

    return jax.shard_map(shards, mesh=mesh, in_specs=in_specs, out_specs=out_specs, check_vma=False)
```
